32 devices in a mesh: rep: 16 (over z, y, x), shard: 2 (over core).
Axes of the slice: x: 2, y: 2, z: 4, core: 2. Of those that a mesh axis runs over, the one named last changes fastest.
Arguments:
- hidden_in: bfloat16 [8192, 768], P(('rep', 'shard')), may hold values from -6 to 6
- cotangent: bfloat16 [8192, 768], P(('rep', 'shard')), may hold values from -6 to 6
- token_count: int32 [32], P(('rep', 'shard')), may hold values from 128 to 256, as said below
- segment_ids: int32 [8192], P(('rep', 'shard')), may hold values from 0 to 255, as said below
- positions: int32 [8192], P(('rep', 'shard')), may hold values from 0 to 255, as said below
- first_gain: bfloat16 [768], P('shard'), may hold values from 0.099609375 to 1.8984375
- first_shift: bfloat16 [768], P('shard'), may hold values from -3 to 3
- second_gain: bfloat16 [768], P('shard'), may hold values from 0.099609375 to 1.8984375
- second_shift: bfloat16 [768], P('shard'), may hold values from -3 to 3
- input_weight: bfloat16 [768, 2304], P('shard'), may hold values from -0.21875 to 0.21875
- input_bias: bfloat16 [2304], P('shard'), may hold values from -3 to 3
- output_weight: bfloat16 [768, 768], P('shard'), may hold values from -0.625 to 0.625
- output_bias: bfloat16 [768], P('shard'), may hold values from -3 to 3
- expand_weight: bfloat16 [768, 3072], P(None, 'shard'), may hold values from -0.21875 to 0.21875
- expand_bias: bfloat16 [3072], P('shard'), may hold values from -3 to 3
- reduce_weight: bfloat16 [3072, 768], P('shard'), may hold values from -0.109375 to 0.109375
- reduce_bias: bfloat16 [768], P('shard'), may hold values from -3 to 3
Outputs:
- block_output: bfloat16 [8192, 768], P(('rep', 'shard'))
- input_gradient: float32 [8192, 768], P(('rep', 'shard'))
- first_gain_gradient: float32 [768], P('shard')
- first_shift_gradient: float32 [768], P('shard')
- second_gain_gradient: float32 [768], P('shard')
- second_shift_gradient: float32 [768], P('shard')
- input_weight_gradient: float32 [768, 2304], P('shard')
- input_bias_gradient: float32 [2304], P('shard')
- output_weight_gradient: float32 [768, 768], P('shard')
- output_bias_gradient: float32 [768], P('shard')
- expand_weight_gradient: float32 [768, 3072], P(None, 'shard')
- expand_bias_gradient: float32 [3072], P('shard')
- reduce_weight_gradient: float32 [3072, 768], P('shard')
- reduce_bias_gradient: float32 [768], P('shard')
The draws below stay inside these ranges and needn't reach their ends.
Inputs may be any that keep to these rules, and one draw needn't show every extreme that they name: `token_count`: each device block holds at least half its slots live; some device has all 256 live and some exactly half. `segment_ids`: within a device block the ids start at 0 and never fall, rising by at most one from slot to slot; some device block has 256 documents of one token. `positions`: A slot's position is its offset from the first slot of its document in its block.
All inputs are finite; a program needn't handle non-finite values.
Results may differ from the reference program's by a relative error of at most 0.017.
Values may be sent and summed in bfloat16 or wider, within the bound.
A program may use at most 128 MiB of HBM per device.

```python
import math
import jax
import jax.numpy as jnp
from jax import lax

D = 768
H = 12
HD = 64
FF = 3072
ROT = 16
TOK_DEV = 256
NDEV = 32
TOKENS = 8192


def layout(key):
    count_key = jax.random.fold_in(key, 11)
    split_key = jax.random.fold_in(key, 12)
    pick_key = jax.random.fold_in(key, 13)
    counts = jax.random.randint(count_key, (NDEV,), TOK_DEV // 2, TOK_DEV + 1)
    chosen = jax.random.randint(pick_key, (3,), 0, NDEV)
    full_device = chosen[0]
    half_device = (full_device + 1 + chosen[1] % (NDEV - 1)) % NDEV
    single_device = (full_device + 1 + chosen[2] % (NDEV - 1)) % NDEV
    device = jnp.arange(NDEV)
    counts = jnp.where(device == half_device, TOK_DEV // 2, counts)
    counts = jnp.where(device == full_device, TOK_DEV, counts)
    slot_index = jnp.arange(TOK_DEV)
    starts_flag = jax.random.randint(split_key, (NDEV, TOK_DEV), 0, TOK_DEV // 3 + 2) == 0
    starts_flag = starts_flag | (slot_index[None, :] == 0)
    starts_flag = starts_flag | (device[:, None] == single_device)
    starts_flag = starts_flag & jnp.logical_not((device[:, None] == full_device) & (slot_index[None, :] > 0))
    segment_table = jnp.cumsum(starts_flag.astype(jnp.int32), axis=1) - 1
    begin_slot = lax.cummax(jnp.where(starts_flag, slot_index[None, :], 0), axis=1)
    position_table = slot_index[None, :] - begin_slot
    return (counts.astype(jnp.int32), segment_table.reshape(-1).astype(jnp.int32), position_table.reshape(-1).astype(jnp.int32))


def draw_token_count(key, part):
    return layout(key)[0]


def draw_segment_ids(key, part):
    return layout(key)[1]


def draw_positions(key, part):
    return layout(key)[2]


def level_of(rng, dims, shards, smallest, largest):
    level = 1.0
    for dim, parts in shards:
        heights = jax.random.uniform(jax.random.fold_in(jax.random.fold_in(rng, 6), dim), (parts,), jnp.float32, smallest / len(shards), largest / len(shards))
        level = level * jnp.repeat(jnp.exp(heights), dims[dim] // parts).reshape((-1,) + (1,) * (len(dims) - 1 - dim))
    return level


def noise(key, dims, scale, limit, shards=(), held_as=jnp.bfloat16):
    factor_of = level_of(key, dims, shards, -0.22, 0.18) if shards else 1.0
    array = jax.random.normal(key, dims, jnp.float32) * scale * factor_of
    return jnp.minimum(jnp.maximum(array, -limit), limit).astype(held_as)


def setup_inputs(seed: int = 0) -> dict:
    splits = jax.random.split(jax.random.key(seed), 18)
    return {
        "hidden_in": noise(splits[0], (TOKENS, D), 1.0, 6.0, ((0, 32),)),
        "cotangent": noise(splits[1], (TOKENS, D), 1.0, 6.0, ((0, 32),)),
        "token_count": draw_token_count(jax.random.fold_in(splits[17], 71), 0),
        "segment_ids": draw_segment_ids(jax.random.fold_in(splits[17], 71), 0),
        "positions": draw_positions(jax.random.fold_in(splits[17], 71), 0),
        "first_gain": jnp.clip(1.0 + 0.18 * jax.random.normal(splits[5], (D,), jnp.float32), 0.099609375, 1.8984375).astype(jnp.bfloat16),
        "first_shift": noise(splits[6], (D,), 0.5, 3.0, ((0, 2),)),
        "second_gain": jnp.clip(1.0 + 0.18 * jax.random.normal(splits[7], (D,), jnp.float32), 0.099609375, 1.8984375).astype(jnp.bfloat16),
        "second_shift": noise(splits[8], (D,), 0.5, 3.0, ((0, 2),)),
        "input_weight": noise(splits[9], (D, 3 * D), D ** -0.5, 0.21875, ((0, 2),)),
        "input_bias": noise(splits[10], (3 * D,), 0.5, 3.0, ((0, 2),)),
        "output_weight": noise(splits[11], (D, D), (D // 8) ** -0.5, 0.625, ((0, 2),)),
        "output_bias": noise(splits[12], (D,), 0.5, 3.0, ((0, 2),)),
        "expand_weight": noise(splits[13], (D, FF), D ** -0.5, 0.21875, ((1, 2),)),
        "expand_bias": noise(splits[14], (FF,), 0.5, 3.0, ((0, 2),)),
        "reduce_weight": noise(splits[15], (FF, D), FF ** -0.5, 0.109375, ((0, 2),)),
        "reduce_bias": noise(splits[16], (D,), 0.5, 3.0, ((0, 2),)),
    }


@jax.custom_vjp
def low(v):
    return lax.optimization_barrier(v.astype(jnp.bfloat16)).astype(jnp.float32)

@jax.custom_vjp
def low_back(v):
    return v

def low_keep(v):
    return (low(v), None)

def low_pass(kept, grad):
    return (grad,)

def back_keep(v):
    return (v, None)

def back_low(kept, grad):
    return (low(grad),)
low.defvjp(low_keep, low_pass)
low_back.defvjp(back_keep, back_low)

def norm_rows(values, gain, shift):
    average = lax.optimization_barrier(jnp.mean(values, axis=-1, keepdims=True))
    centred = values - average
    variance = lax.optimization_barrier(jnp.mean(centred * centred, axis=-1, keepdims=True))
    return centred * lax.rsqrt(variance + 1e-05) * gain + shift

def rotate(block, cosine_table, sine_table):
    halfway = ROT // 2
    lower = block[..., :halfway]
    upper = block[..., halfway:ROT]
    return jnp.concatenate([lower * cosine_table - upper * sine_table, upper * cosine_table + lower * sine_table, block[..., ROT:]], axis=-1)

def device_block(parameters, block_item):
    rows, segment_row, position_row, live_count = block_item
    gain_one, shift_one, gain_two, shift_two, joint_weight, joint_bias, proj_weight, proj_bias, wide_weight, wide_bias, narrow_weight, narrow_bias = parameters
    highest = lax.Precision.HIGHEST
    normed_one = low(norm_rows(rows, gain_one, shift_one))
    normed_two = low(norm_rows(rows, gain_two, shift_two))
    joined = low_back(jnp.dot(normed_one, joint_weight, precision=highest) + joint_bias)
    halfway = ROT // 2
    frequency = 10000.0 ** (-jnp.arange(halfway, dtype=jnp.float32) * 2.0 / ROT)
    angles = position_row.astype(jnp.float32)[:, None] * frequency[None, :]
    cosine_table = jnp.cos(angles)[:, None, :]
    sine_table = jnp.sin(angles)[:, None, :]
    queries = low(rotate(joined[:, :D].reshape(TOK_DEV, H, HD), cosine_table, sine_table))
    key_rows = low(rotate(joined[:, D:2 * D].reshape(TOK_DEV, H, HD), cosine_table, sine_table))
    value_rows = low(joined[:, 2 * D:].reshape(TOK_DEV, H, HD))
    raw_scores = low_back(jnp.einsum('qhd,khd->hqk', queries, key_rows, precision=highest) * (1.0 / math.sqrt(HD)))
    slot_index = jnp.arange(TOK_DEV)
    live_rows = slot_index < live_count
    allowed = (segment_row[:, None] == segment_row[None, :]) & (slot_index[None, :] <= slot_index[:, None]) & live_rows[None, :]
    allowed = allowed | (slot_index[:, None] == slot_index[None, :])
    scores = jnp.where(allowed[None], raw_scores, -1e+30)
    probability = low(jax.nn.softmax(scores, axis=-1))
    mixed = jnp.einsum('hqk,khd->qhd', probability, value_rows, precision=highest).reshape(TOK_DEV, D)
    mixed = low(low_back(mixed))
    attention = low_back(jnp.dot(mixed, proj_weight, precision=highest) + proj_bias)
    expanded = low_back(jnp.dot(normed_two, wide_weight, precision=highest) + wide_bias)
    activated = low(jax.nn.gelu(expanded, approximate=False))
    forward_feed = low_back(jnp.dot(activated, narrow_weight, precision=highest) + narrow_bias)
    return live_rows.astype(jnp.float32)[:, None] * (rows + attention + forward_feed)

def reference(hidden_in, cotangent, token_count, segment_ids, positions, first_gain, first_shift, second_gain, second_shift, input_weight, input_bias, output_weight, output_bias, expand_weight, expand_bias, reduce_weight, reduce_bias):
    parameters = (first_gain.astype(jnp.float32), first_shift.astype(jnp.float32), second_gain.astype(jnp.float32), second_shift.astype(jnp.float32), input_weight.astype(jnp.float32), input_bias.astype(jnp.float32), output_weight.astype(jnp.float32), output_bias.astype(jnp.float32), expand_weight.astype(jnp.float32), expand_bias.astype(jnp.float32), reduce_weight.astype(jnp.float32), reduce_bias.astype(jnp.float32))
    blocks = hidden_in.astype(jnp.float32).reshape(NDEV, TOK_DEV, D)
    segment_blocks = segment_ids.reshape(NDEV, TOK_DEV)
    position_blocks = positions.reshape(NDEV, TOK_DEV)

    def forward(blocks, parameters):

        def one_device(block_item):
            return device_block(parameters, block_item)
        return lax.map(jax.checkpoint(one_device), (blocks, segment_blocks, position_blocks, token_count))
    result, pullback = jax.vjp(forward, blocks, parameters)
    block_grad, grads = pullback(cotangent.astype(jnp.float32).reshape(NDEV, TOK_DEV, D))
    return (result.reshape(TOKENS, D).astype(jnp.bfloat16), block_grad.reshape(TOKENS, D), grads[0], grads[1], grads[2], grads[3], grads[4], grads[5], grads[6], grads[7], grads[8], grads[9], grads[10], grads[11])
```

```python
import math

import jax
import jax.numpy as jnp
from jax import lax
from jax.sharding import PartitionSpec as P

D = 768
H = 12
HD = 64
ROT = 16


epsilon = 1e-05


def norm_rows(values, gain, shift):
    average = jnp.mean(values, axis=-1, keepdims=True)
    centred = values - average
    variance = jnp.mean(centred * centred, axis=-1, keepdims=True)
    return centred * lax.rsqrt(variance + epsilon) * gain + shift


def rotate(block, cosine_table, sine_table):
    halfway = ROT // 2
    lower = block[..., :halfway]
    upper = block[..., halfway:ROT]
    return jnp.concatenate(
        [
            lower * cosine_table - upper * sine_table,
            upper * cosine_table + lower * sine_table,
            block[..., ROT:],
        ],
        axis=-1,
    )


def transposed_right(left, right):
    return lax.dot_general(
        left, right, (((1,), (1,)), ((), ())), preferred_element_type=jnp.float32
    )


def transposed_left(left, right):
    return lax.dot_general(
        left, right, (((0,), (0,)), ((), ())), preferred_element_type=jnp.float32
    )


def exact_gelu(values):
    return jax.nn.gelu(values, approximate=False)


def partner_parts(block, count):
    parts = [block]
    for step in range(1, count):
        pairs = [((index + step) % count, index) for index in range(count)]
        parts.append(lax.ppermute(block, "shard", pairs))
    return parts


def to_owner(parts, count):
    total = parts[0]
    for step in range(1, count):
        pairs = [(index, (index + step) % count) for index in range(count)]
        arrived = lax.ppermute(parts[step].astype(jnp.bfloat16), "shard", pairs)
        total = total + arrived.astype(jnp.float32)
    return total.astype(jnp.bfloat16)


def natural(parts, count, mine):
    width = parts[0].shape[1]
    if count == 2:
        return jnp.concatenate(
            [
                jnp.where(mine == 0, parts[0], parts[1]),
                jnp.where(mine == 0, parts[1], parts[0]),
            ],
            axis=1,
        )
    twice = jnp.concatenate(list(parts) + list(parts), axis=1)
    start = lax.rem(count - mine, count) * width
    return lax.dynamic_slice_in_dim(twice, start, count * width, axis=1)


def rep_total(block, order, replicas, mine):
    kept_bits = []
    for bit in order:
        pairs = [(index, index ^ (1 << bit)) for index in range(replicas)]
        side = lax.rem(lax.div(mine, 1 << bit), 2)
        half = block.shape[0] // 2
        outgoing = lax.dynamic_slice_in_dim(block, (1 - side) * half, half, axis=0)
        kept = lax.dynamic_slice_in_dim(block, side * half, half, axis=0)
        arrived = lax.ppermute(outgoing, "rep", pairs)
        block = (kept.astype(jnp.float32) + arrived.astype(jnp.float32)).astype(jnp.bfloat16)
        kept_bits.append((side, pairs))
    for side, pairs in reversed(kept_bits):
        arrived = lax.ppermute(block, "rep", pairs)
        block = jnp.concatenate(
            [jnp.where(side == 0, block, arrived), jnp.where(side == 0, arrived, block)],
            axis=0,
        )
    return block


def make_shards(replicas, count):
    bits = replicas.bit_length() - 1
    orders = (tuple(range(bits)), (1, 0) + tuple(range(2, bits)))

    def shards(
        hidden_in,
        cotangent,
        token_count,
        segment_ids,
        positions,
        first_gain,
        first_shift,
        second_gain,
        second_shift,
        input_weight,
        input_bias,
        output_weight,
        output_bias,
        expand_weight,
        expand_bias,
        reduce_weight,
        reduce_bias,
    ):
        row_count = hidden_in.shape[0]
        mine = lax.axis_index("shard")
        replica = lax.axis_index("rep")
        own = hidden_in.shape[1] // count
        owned_vectors = [
            first_gain,
            first_shift,
            second_gain,
            second_shift,
            input_bias,
            output_bias,
            reduce_bias,
            expand_bias,
        ]
        vector_sizes = [vector.shape[0] for vector in owned_vectors]
        vector_parts = partner_parts(jnp.concatenate(owned_vectors)[None, :], count)
        wide_parts = partner_parts(expand_weight, count)
        narrow_parts = partner_parts(reduce_weight, count)
        joint_parts = partner_parts(input_weight, count)
        proj_parts = partner_parts(output_weight, count)

        def vector_of(place):
            begin = sum(vector_sizes[:place])
            pieces = [part[:, begin : begin + vector_sizes[place]] for part in vector_parts]
            return pieces

        whole_vectors = [natural(vector_of(place), count, mine)[0] for place in range(7)]
        (
            gain_one,
            shift_one,
            gain_two,
            shift_two,
            joint_bias,
            proj_bias,
            narrow_bias,
        ) = [vector.astype(jnp.float32) for vector in whole_vectors]
        wide_bias_parts = [piece.astype(jnp.float32) for piece in vector_of(7)]

        values = hidden_in.astype(jnp.float32)
        slot_index = jnp.arange(row_count)
        live_rows = slot_index < token_count[0]
        live_mask = live_rows.astype(jnp.float32)[:, None]
        normed_one, first_pull = jax.vjp(norm_rows, values, gain_one, shift_one)
        normed_two, second_pull = jax.vjp(norm_rows, values, gain_two, shift_two)
        first_low = normed_one.astype(jnp.bfloat16)
        second_low = normed_two.astype(jnp.bfloat16)
        grad_rows = cotangent.astype(jnp.float32) * live_mask
        grad_low = grad_rows.astype(jnp.bfloat16)
        bias_sum = jnp.sum(grad_rows, axis=0)

        def column_halves(block):
            half = block.shape[1] // 2
            return (block[:, :half], block[:, half:])

        def reduced(left_parts, right_parts):
            outcome = []
            for half, order in enumerate(orders):
                terms = [
                    transposed_left(left, column_halves(right)[half])
                    for left, right in zip(left_parts, right_parts)
                ]
                outcome.append(
                    rep_total(to_owner(terms, count), order, replicas, replica)
                )
            return jnp.concatenate(outcome, axis=1).astype(jnp.float32)

        forward_feed = narrow_bias[None, :]
        activated_parts = []
        expanded_grad_parts = []
        second_grad = None
        for wide, narrow, bias in zip(wide_parts, narrow_parts, wide_bias_parts):
            expanded = jnp.dot(second_low, wide, preferred_element_type=jnp.float32) + bias
            activated_full, expand_pull = jax.vjp(exact_gelu, expanded)
            activated = activated_full.astype(jnp.bfloat16)
            forward_feed = forward_feed + jnp.dot(
                activated, narrow, preferred_element_type=jnp.float32
            )
            hidden_grad = transposed_right(grad_low, narrow)
            expanded_grad = expand_pull(hidden_grad)[0].astype(jnp.bfloat16)
            part_grad = transposed_right(expanded_grad, wide)
            second_grad = part_grad if second_grad is None else second_grad + part_grad
            activated_parts.append(activated)
            expanded_grad_parts.append(expanded_grad)
        total_narrow = reduced(activated_parts, [grad_low] * count)
        total_wide = reduced([second_low] * count, expanded_grad_parts)
        wide_bias_grad = natural(
            [
                jnp.sum(part, axis=0, dtype=jnp.float32)[None, :]
                for part in expanded_grad_parts
            ],
            count,
            mine,
        )[0]

        def feature_parts(block):
            if count == 2:
                lower, upper = block[:, :own], block[:, own:]
                return [
                    jnp.where(mine == 0, lower, upper),
                    jnp.where(mine == 0, upper, lower),
                ]
            return [
                lax.dynamic_slice_in_dim(
                    block, lax.rem(mine + step, count) * own, own, axis=1
                )
                for step in range(count)
            ]

        first_parts = feature_parts(first_low)
        joined = joint_bias[None, :]
        for part, weight in zip(first_parts, joint_parts):
            joined = joined + jnp.dot(part, weight, preferred_element_type=jnp.float32)
        halfway = ROT // 2
        frequency = 10000.0 ** (-jnp.arange(halfway, dtype=jnp.float32) * 2.0 / ROT)
        angles = positions.astype(jnp.float32)[:, None] * frequency[None, :]
        cosine_table = jnp.cos(angles)[:, None, :]
        sine_table = jnp.sin(angles)[:, None, :]
        queries = rotate(
            joined[:, :D].reshape(row_count, H, HD), cosine_table, sine_table
        ).astype(jnp.bfloat16)
        key_rows = rotate(
            joined[:, D : 2 * D].reshape(row_count, H, HD), cosine_table, sine_table
        ).astype(jnp.bfloat16)
        value_rows = joined[:, 2 * D :].reshape(row_count, H, HD).astype(jnp.bfloat16)
        score_scale = 1.0 / math.sqrt(HD)
        allowed = (
            (segment_ids[:, None] == segment_ids[None, :])
            & (slot_index[None, :] <= slot_index[:, None])
            & live_rows[None, :]
        )
        allowed = allowed | (slot_index[:, None] == slot_index[None, :])
        raw_scores = (
            jnp.einsum("qhd,khd->hqk", queries, key_rows, preferred_element_type=jnp.float32)
            * score_scale
        )
        scores = jnp.where(allowed[None], raw_scores, -1e30)
        row_top = jnp.max(scores, axis=-1, keepdims=True)
        exponent = jnp.exp(scores - row_top)
        row_total = jnp.sum(exponent, axis=-1, keepdims=True)
        probability = exponent / row_total
        probability_low = probability.astype(jnp.bfloat16)
        mixed_low = (
            jnp.einsum(
                "hqk,khd->qhd", probability_low, value_rows, preferred_element_type=jnp.float32
            )
            .reshape(row_count, D)
            .astype(jnp.bfloat16)
        )
        mixed_parts = feature_parts(mixed_low)
        attention = proj_bias[None, :]
        for part, weight in zip(mixed_parts, proj_parts):
            attention = attention + jnp.dot(part, weight, preferred_element_type=jnp.float32)
        block_output = (live_mask * (values + attention + forward_feed)).astype(jnp.bfloat16)
        total_proj = reduced(mixed_parts, [grad_low] * count)
        mixed_grad = natural(
            [transposed_right(grad_low, weight).astype(jnp.bfloat16) for weight in proj_parts],
            count,
            mine,
        ).reshape(row_count, H, HD)
        prob_grad = jnp.einsum(
            "qhd,khd->hqk", mixed_grad, value_rows, preferred_element_type=jnp.float32
        )
        value_grad = jnp.einsum(
            "hqk,qhd->khd", probability_low, mixed_grad, preferred_element_type=jnp.float32
        )
        inner_sum = jnp.sum(prob_grad * probability, axis=-1, keepdims=True)
        score_grad = (probability * (prob_grad - inner_sum)).astype(jnp.bfloat16)
        query_grad = (
            jnp.einsum("hqk,khd->qhd", score_grad, key_rows, preferred_element_type=jnp.float32)
            * score_scale
        )
        key_grad = (
            jnp.einsum("hqk,qhd->khd", score_grad, queries, preferred_element_type=jnp.float32)
            * score_scale
        )
        query_grad = rotate(query_grad, cosine_table, -sine_table)
        key_grad = rotate(key_grad, cosine_table, -sine_table)
        joined_grad = jnp.concatenate(
            [
                query_grad.reshape(row_count, D),
                key_grad.reshape(row_count, D),
                value_grad.reshape(row_count, D),
            ],
            axis=1,
        ).astype(jnp.bfloat16)
        joint_bias_grad = jnp.sum(joined_grad, axis=0, dtype=jnp.float32)
        total_joint = reduced(first_parts, [joined_grad] * count)
        first_grad = natural(
            [transposed_right(joined_grad, weight) for weight in joint_parts], count, mine
        )
        first_input, gain_one_grad, shift_one_grad = first_pull(first_grad)
        second_input, gain_two_grad, shift_two_grad = second_pull(second_grad)
        input_gradient = grad_rows + first_input + second_input
        sums = [
            gain_one_grad,
            shift_one_grad,
            gain_two_grad,
            shift_two_grad,
            joint_bias_grad,
            bias_sum,
            wide_bias_grad,
        ]
        sum_sizes = [item.shape[0] for item in sums]
        joined_sums = jnp.concatenate(sums).reshape(-1, 128)
        for axis, size in (("shard", count), ("rep", replicas)):
            for bit in range(size.bit_length() - 1):
                pairs = [(index, index ^ (1 << bit)) for index in range(size)]
                joined_sums = joined_sums + lax.ppermute(joined_sums, axis, pairs)
        joined_sums = joined_sums.reshape(-1)
        owned = []
        begin = 0
        for size in sum_sizes:
            share = size // count
            owned.append(
                lax.dynamic_slice_in_dim(joined_sums, begin + mine * share, share, axis=0)
            )
            begin += size
        return (
            block_output,
            input_gradient,
            owned[0],
            owned[1],
            owned[2],
            owned[3],
            total_joint,
            owned[4],
            total_proj,
            owned[5],
            total_wide,
            owned[6],
            total_narrow,
            owned[5],
        )

    return shards


def solution(mesh):
    return jax.shard_map(
        make_shards(mesh.shape["rep"], mesh.shape["shard"]),
        mesh=mesh,
        in_specs=(
            P(("rep", "shard"), None),
            P(("rep", "shard"), None),
            P(("rep", "shard")),
            P(("rep", "shard")),
            P(("rep", "shard")),
            P("shard"),
            P("shard"),
            P("shard"),
            P("shard"),
            P("shard", None),
            P("shard"),
            P("shard", None),
            P("shard"),
            P(None, "shard"),
            P("shard"),
            P("shard", None),
            P("shard"),
        ),
        out_specs=(
            P(("rep", "shard"), None),
            P(("rep", "shard"), None),
            P("shard"),
            P("shard"),
            P("shard"),
            P("shard"),
            P("shard", None),
            P("shard"),
            P("shard", None),
            P("shard"),
            P(None, "shard"),
            P("shard"),
            P("shard", None),
            P("shard"),
        ),
        check_vma=False,
    )
```

```python
import functools
import math

import jax
import jax.numpy as jnp
from jax import lax
from jax.experimental import pallas as pl
from jax.experimental.pallas import tpu as pltpu
from jax.sharding import PartitionSpec as P

D = 768
H = 12
HD = 64
ROT = 16


epsilon = 1e-05


def norm_rows(values, gain, shift):
    average = jnp.mean(values, axis=-1, keepdims=True)
    centred = values - average
    variance = jnp.mean(centred * centred, axis=-1, keepdims=True)
    return centred * lax.rsqrt(variance + epsilon) * gain + shift


def rotate(block, cosine_table, sine_table):
    halfway = ROT // 2
    lower = block[..., :halfway]
    upper = block[..., halfway:ROT]
    return jnp.concatenate(
        [
            lower * cosine_table - upper * sine_table,
            upper * cosine_table + lower * sine_table,
            block[..., ROT:],
        ],
        axis=-1,
    )


def transposed_right(left, right):
    return lax.dot_general(
        left, right, (((1,), (1,)), ((), ())), preferred_element_type=jnp.float32
    )


def transposed_left(left, right):
    return lax.dot_general(
        left, right, (((0,), (0,)), ((), ())), preferred_element_type=jnp.float32
    )


def exact_gelu(values):
    return jax.nn.gelu(values, approximate=False)


def partner_parts(block, count):
    parts = [block]
    for step in range(1, count):
        pairs = [((index + step) % count, index) for index in range(count)]
        parts.append(lax.ppermute(block, "shard", pairs))
    return parts


def natural(parts, count, mine):
    width = parts[0].shape[1]
    if count == 2:
        return jnp.concatenate(
            [
                jnp.where(mine == 0, parts[0], parts[1]),
                jnp.where(mine == 0, parts[1], parts[0]),
            ],
            axis=1,
        )
    twice = jnp.concatenate(list(parts) + list(parts), axis=1)
    start = lax.rem(count - mine, count) * width
    return lax.dynamic_slice_in_dim(twice, start, count * width, axis=1)


def add_rows(target, target_at, first, first_at, second, rows):
    step = math.gcd(rows, 48)

    def body(turn, carry):
        offset = turn * step
        left = first[pl.ds(pl.multiple_of(first_at + offset, 16), step), :]
        right = second[pl.ds(pl.multiple_of(offset, 16), step), :]
        target[pl.ds(pl.multiple_of(target_at + offset, 16), step), :] = (
            left.astype(jnp.float32) + right.astype(jnp.float32)
        ).astype(target.dtype)
        return carry

    lax.fori_loop(0, rows // step, body, 0)


def sum_kernel(bits, groups, own_ref, other_ref, vec_ref, out_ref, vec_out_ref, *scratch):
    held = scratch[0]
    landing = scratch[1 : 1 + bits]
    vec_held, vec_landing, send_sem, recv_sem, vec_send, vec_recv = scratch[1 + bits :]
    rep = lax.axis_index("rep")
    core = lax.axis_index("shard")
    chunks, rows, _ = out_ref.shape
    sides = [lax.rem(lax.div(rep, 1 << bit), 2) for bit in range(bits)]
    peers = [(rep + (1 << bit) * (1 - 2 * sides[bit]), core) for bit in range(bits)]
    twin = (rep, 1 - core)

    barrier = pltpu.get_barrier_semaphore()
    for device in [twin] + peers:
        pl.semaphore_signal(
            barrier, inc=1, device_id=device, device_id_type=pl.DeviceIdType.MESH
        )
    pl.semaphore_wait(barrier, 1 + bits)

    def order_of(chunk):
        return groups[chunk]

    def region(chunk, depth):
        start = 0
        for place in range(depth):
            start = start + sides[order_of(chunk)[place]] * (rows >> (place + 1))
        return start

    copies = {}

    def launch(chunk, stage, source, target, device):
        copy = pltpu.make_async_remote_copy(
            src_ref=source,
            dst_ref=target,
            send_sem=send_sem.at[chunk, stage],
            recv_sem=recv_sem.at[chunk, stage],
            device_id=device,
            device_id_type=pl.DeviceIdType.MESH,
        )
        copy.start()
        copies[chunk, stage] = copy

    def rows_of(ref, chunk, start, size):
        return ref.at[chunk, pl.ds(pl.multiple_of(start, 16), size), :]

    def advance(chunk, stage):
        if stage == 0:
            launch(chunk, 0, other_ref.at[chunk], held.at[chunk], twin)
            return
        copies[chunk, stage - 1].wait()
        if stage <= bits + 1:
            depth = stage - 1
            size = rows >> depth
            here = region(chunk, depth)
            goal = held if stage <= bits else out_ref
            if depth == 0:
                add_rows(held.at[chunk], 0, held.at[chunk], 0, own_ref.at[chunk], rows)
            else:
                add_rows(
                    goal.at[chunk],
                    here,
                    held.at[chunk],
                    here,
                    landing[depth - 1].at[chunk],
                    size,
                )
        if stage <= bits:
            bit = order_of(chunk)[stage - 1]
            half = rows >> stage
            away = region(chunk, stage - 1) + (1 - sides[bit]) * half
            launch(
                chunk,
                stage,
                rows_of(held, chunk, away, half),
                landing[stage - 1].at[chunk],
                peers[bit],
            )
        elif stage <= 2 * bits:
            depth = 2 * bits + 1 - stage
            bit = order_of(chunk)[depth - 1]
            block = rows_of(out_ref, chunk, region(chunk, depth), rows >> depth)
            launch(chunk, stage, block, block, peers[bit])

    vec_copies = {}

    def advance_vector(stage):
        if stage > 0:
            vec_copies[stage - 1].wait()
            source = vec_ref if stage == 1 else vec_held.at[stage - 2]
            goal = vec_out_ref if stage == bits + 1 else vec_held.at[stage - 1]
            goal[...] = source[...] + vec_landing[stage - 1]
        if stage <= bits:
            copy = pltpu.make_async_remote_copy(
                src_ref=vec_ref if stage == 0 else vec_held.at[stage - 1],
                dst_ref=vec_landing.at[stage],
                send_sem=vec_send.at[stage],
                recv_sem=vec_recv.at[stage],
                device_id=twin if stage == 0 else peers[stage - 1],
                device_id_type=pl.DeviceIdType.MESH,
            )
            copy.start()
            vec_copies[stage] = copy

    turns = []
    for chunk in range(chunks):
        for stage in range(2 * bits + 2):
            turns.append((stage + (chunk // 2 if stage else 0), chunk, stage))
    for stage in range(bits + 2):
        turns.append((stage, chunks, stage))
    for _, chunk, stage in sorted(turns):
        if chunk == chunks:
            advance_vector(stage)
        else:
            advance(chunk, stage)


def summed(own_rows, other_rows, vector, replicas):
    width = own_rows.shape[1]
    rows = width
    chunks = own_rows.shape[0] // rows
    bits = replicas.bit_length() - 1
    forward = tuple(range(bits))
    swapped = (1, 0) + forward[2:]
    groups = tuple(forward if chunk % 2 == 0 else swapped for chunk in range(chunks))
    stages = 2 * bits + 1
    vmem = pl.BlockSpec(memory_space=pltpu.VMEM)
    landing = [
        pltpu.VMEM((chunks, rows >> (bit + 1), width), jnp.bfloat16) for bit in range(bits)
    ]
    totals, vector_total = pl.pallas_call(
        functools.partial(sum_kernel, bits, groups),
        out_shape=(
            jax.ShapeDtypeStruct((chunks, rows, width), jnp.bfloat16),
            jax.ShapeDtypeStruct(vector.shape, jnp.float32),
        ),
        in_specs=[vmem, pl.BlockSpec(memory_space=pl.ANY), vmem],
        out_specs=(vmem, vmem),
        scratch_shapes=[pltpu.VMEM((chunks, rows, width), jnp.bfloat16)]
        + landing
        + [
            pltpu.VMEM((bits,) + vector.shape, jnp.float32),
            pltpu.VMEM((bits + 1,) + vector.shape, jnp.float32),
            pltpu.SemaphoreType.DMA((chunks, stages)),
            pltpu.SemaphoreType.DMA((chunks, stages)),
            pltpu.SemaphoreType.DMA((bits + 1,)),
            pltpu.SemaphoreType.DMA((bits + 1,)),
        ],
        compiler_params=pltpu.CompilerParams(
            collective_id=0, has_side_effects=True, vmem_limit_bytes=52 * 2**20
        ),
    )(
        own_rows.reshape(chunks, rows, width),
        other_rows.reshape(chunks, rows, width),
        vector,
    )
    return totals.reshape(chunks * rows, width), vector_total


def scattered(gradient, axis):
    owned = lax.psum_scatter(
        gradient.astype(jnp.bfloat16), "shard", scatter_dimension=axis, tiled=True
    )
    return lax.psum(owned, "rep").astype(jnp.float32)


def make_shards(replicas, count):
    def shards(
        hidden_in,
        cotangent,
        token_count,
        segment_ids,
        positions,
        first_gain,
        first_shift,
        second_gain,
        second_shift,
        input_weight,
        input_bias,
        output_weight,
        output_bias,
        expand_weight,
        expand_bias,
        reduce_weight,
        reduce_bias,
    ):
        row_count = hidden_in.shape[0]
        mine = lax.axis_index("shard")
        replica = lax.axis_index("rep")
        own = hidden_in.shape[1] // count
        owned_vectors = [
            first_gain,
            first_shift,
            second_gain,
            second_shift,
            input_bias,
            output_bias,
            reduce_bias,
            expand_bias,
        ]
        vector_sizes = [vector.shape[0] for vector in owned_vectors]
        vector_parts = partner_parts(jnp.concatenate(owned_vectors)[None, :], count)
        wide_parts = partner_parts(expand_weight, count)
        narrow_parts = partner_parts(reduce_weight, count)
        joint_parts = partner_parts(input_weight, count)
        proj_parts = partner_parts(output_weight, count)

        def vector_of(place):
            begin = sum(vector_sizes[:place])
            pieces = [part[:, begin : begin + vector_sizes[place]] for part in vector_parts]
            return pieces

        whole_vectors = [natural(vector_of(place), count, mine)[0] for place in range(7)]
        (
            gain_one,
            shift_one,
            gain_two,
            shift_two,
            joint_bias,
            proj_bias,
            narrow_bias,
        ) = [vector.astype(jnp.float32) for vector in whole_vectors]
        wide_bias_parts = [piece.astype(jnp.float32) for piece in vector_of(7)]

        values = hidden_in.astype(jnp.float32)
        slot_index = jnp.arange(row_count)
        live_rows = slot_index < token_count[0]
        live_mask = live_rows.astype(jnp.float32)[:, None]
        normed_one, first_pull = jax.vjp(norm_rows, values, gain_one, shift_one)
        normed_two, second_pull = jax.vjp(norm_rows, values, gain_two, shift_two)
        first_low = normed_one.astype(jnp.bfloat16)
        second_low = normed_two.astype(jnp.bfloat16)
        grad_rows = cotangent.astype(jnp.float32) * live_mask
        grad_low = grad_rows.astype(jnp.bfloat16)
        bias_sum = jnp.sum(grad_rows, axis=0)

        width = hidden_in.shape[1]
        paired = count == 2 and replicas >= 4 and width % (16 * replicas) == 0
        paired = paired and replicas & (replicas - 1) == 0

        def stacked(left, right):
            return [
                transposed_left(left, right[:, begin : begin + width]).astype(jnp.bfloat16)
                for begin in range(0, right.shape[1], width)
            ]

        forward_feed = narrow_bias[None, :]
        activated_parts = []
        expanded_grad_parts = []
        second_grad = None
        for wide, narrow, bias in zip(wide_parts, narrow_parts, wide_bias_parts):
            expanded = jnp.dot(second_low, wide, preferred_element_type=jnp.float32) + bias
            activated_full, expand_pull = jax.vjp(exact_gelu, expanded)
            activated = activated_full.astype(jnp.bfloat16)
            forward_feed = forward_feed + jnp.dot(
                activated, narrow, preferred_element_type=jnp.float32
            )
            hidden_grad = transposed_right(grad_low, narrow)
            expanded_grad = expand_pull(hidden_grad)[0].astype(jnp.bfloat16)
            part_grad = transposed_right(expanded_grad, wide)
            second_grad = part_grad if second_grad is None else second_grad + part_grad
            activated_parts.append(activated)
            expanded_grad_parts.append(expanded_grad)
        wide_bias_grad = natural(
            [
                jnp.sum(part, axis=0, dtype=jnp.float32)[None, :]
                for part in expanded_grad_parts
            ],
            count,
            mine,
        )[0]

        def feature_parts(block):
            if count == 2:
                lower, upper = block[:, :own], block[:, own:]
                return [
                    jnp.where(mine == 0, lower, upper),
                    jnp.where(mine == 0, upper, lower),
                ]
            return [
                lax.dynamic_slice_in_dim(
                    block, lax.rem(mine + step, count) * own, own, axis=1
                )
                for step in range(count)
            ]

        first_parts = feature_parts(first_low)
        joined = joint_bias[None, :]
        for part, weight in zip(first_parts, joint_parts):
            joined = joined + jnp.dot(part, weight, preferred_element_type=jnp.float32)
        halfway = ROT // 2
        frequency = 10000.0 ** (-jnp.arange(halfway, dtype=jnp.float32) * 2.0 / ROT)
        angles = positions.astype(jnp.float32)[:, None] * frequency[None, :]
        cosine_table = jnp.cos(angles)[:, None, :]
        sine_table = jnp.sin(angles)[:, None, :]
        queries = rotate(
            joined[:, :D].reshape(row_count, H, HD), cosine_table, sine_table
        ).astype(jnp.bfloat16)
        key_rows = rotate(
            joined[:, D : 2 * D].reshape(row_count, H, HD), cosine_table, sine_table
        ).astype(jnp.bfloat16)
        value_rows = joined[:, 2 * D :].reshape(row_count, H, HD).astype(jnp.bfloat16)
        score_scale = 1.0 / math.sqrt(HD)
        allowed = (
            (segment_ids[:, None] == segment_ids[None, :])
            & (slot_index[None, :] <= slot_index[:, None])
            & live_rows[None, :]
        )
        allowed = allowed | (slot_index[:, None] == slot_index[None, :])
        raw_scores = (
            jnp.einsum("qhd,khd->hqk", queries, key_rows, preferred_element_type=jnp.float32)
            * score_scale
        )
        scores = jnp.where(allowed[None], raw_scores, -1e30)
        row_top = jnp.max(scores, axis=-1, keepdims=True)
        exponent = jnp.exp(scores - row_top)
        row_total = jnp.sum(exponent, axis=-1, keepdims=True)
        probability = exponent / row_total
        probability_low = probability.astype(jnp.bfloat16)
        mixed_low = (
            jnp.einsum(
                "hqk,khd->qhd", probability_low, value_rows, preferred_element_type=jnp.float32
            )
            .reshape(row_count, D)
            .astype(jnp.bfloat16)
        )
        mixed_parts = feature_parts(mixed_low)
        attention = proj_bias[None, :]
        for part, weight in zip(mixed_parts, proj_parts):
            attention = attention + jnp.dot(part, weight, preferred_element_type=jnp.float32)
        block_output = (live_mask * (values + attention + forward_feed)).astype(jnp.bfloat16)
        mixed_grad = natural(
            [transposed_right(grad_low, weight).astype(jnp.bfloat16) for weight in proj_parts],
            count,
            mine,
        ).reshape(row_count, H, HD)
        prob_grad = jnp.einsum(
            "qhd,khd->hqk", mixed_grad, value_rows, preferred_element_type=jnp.float32
        )
        value_grad = jnp.einsum(
            "hqk,qhd->khd", probability_low, mixed_grad, preferred_element_type=jnp.float32
        )
        inner_sum = jnp.sum(prob_grad * probability, axis=-1, keepdims=True)
        score_grad = (probability * (prob_grad - inner_sum)).astype(jnp.bfloat16)
        query_grad = (
            jnp.einsum("hqk,khd->qhd", score_grad, key_rows, preferred_element_type=jnp.float32)
            * score_scale
        )
        key_grad = (
            jnp.einsum("hqk,qhd->khd", score_grad, queries, preferred_element_type=jnp.float32)
            * score_scale
        )
        query_grad = rotate(query_grad, cosine_table, -sine_table)
        key_grad = rotate(key_grad, cosine_table, -sine_table)
        joined_grad = jnp.concatenate(
            [
                query_grad.reshape(row_count, D),
                key_grad.reshape(row_count, D),
                value_grad.reshape(row_count, D),
            ],
            axis=1,
        ).astype(jnp.bfloat16)
        joint_bias_grad = jnp.sum(joined_grad, axis=0, dtype=jnp.float32)
        first_grad = natural(
            [transposed_right(joined_grad, weight) for weight in joint_parts], count, mine
        )
        first_input, gain_one_grad, shift_one_grad = first_pull(first_grad)
        second_input, gain_two_grad, shift_two_grad = second_pull(second_grad)
        input_gradient = grad_rows + first_input + second_input
        sums = [
            gain_one_grad,
            shift_one_grad,
            gain_two_grad,
            shift_two_grad,
            joint_bias_grad,
            bias_sum,
            wide_bias_grad,
        ]
        sum_sizes = [item.shape[0] for item in sums]
        joined_sums = jnp.concatenate(sums).reshape(-1, 128)
        if paired:
            sent = [
                jnp.concatenate(
                    stacked(activated_parts[part], grad_low)
                    + stacked(second_low, expanded_grad_parts[part])
                    + stacked(first_parts[part], joined_grad)
                    + stacked(mixed_parts[part], grad_low),
                    axis=0,
                )
                for part in range(count)
            ]
            totals, joined_sums = summed(sent[0], sent[1], joined_sums, replicas)
            totals = totals.astype(jnp.float32)
            place = 0

            def taken(tall, broad):
                nonlocal place
                pieces = []
                for _ in range(broad // width):
                    pieces.append(totals[place : place + tall])
                    place += tall
                return pieces[0] if len(pieces) == 1 else jnp.concatenate(pieces, axis=1)

            total_narrow = taken(*reduce_weight.shape)
            total_wide = taken(*expand_weight.shape)
            total_joint = taken(*input_weight.shape)
            total_proj = taken(*output_weight.shape)
        else:
            activated = natural(activated_parts, count, mine)
            expanded_grad = natural(expanded_grad_parts, count, mine)
            total_narrow = scattered(transposed_left(activated, grad_low), 0)
            total_wide = scattered(transposed_left(second_low, expanded_grad), 1)
            total_joint = scattered(transposed_left(first_low, joined_grad), 0)
            total_proj = scattered(transposed_left(mixed_low, grad_low), 0)
            joined_sums = lax.psum(joined_sums, ("rep", "shard"))
        joined_sums = joined_sums.reshape(-1)
        owned = []
        begin = 0
        for size in sum_sizes:
            share = size // count
            owned.append(
                lax.dynamic_slice_in_dim(joined_sums, begin + mine * share, share, axis=0)
            )
            begin += size
        return (
            block_output,
            input_gradient,
            owned[0],
            owned[1],
            owned[2],
            owned[3],
            total_joint,
            owned[4],
            total_proj,
            owned[5],
            total_wide,
            owned[6],
            total_narrow,
            owned[5],
        )

    return shards


def solution(mesh):
    return jax.shard_map(
        make_shards(mesh.shape["rep"], mesh.shape["shard"]),
        mesh=mesh,
        in_specs=(
            P(("rep", "shard"), None),
            P(("rep", "shard"), None),
            P(("rep", "shard")),
            P(("rep", "shard")),
            P(("rep", "shard")),
            P("shard"),
            P("shard"),
            P("shard"),
            P("shard"),
            P("shard", None),
            P("shard"),
            P("shard", None),
            P("shard"),
            P(None, "shard"),
            P("shard"),
            P("shard", None),
            P("shard"),
        ),
        out_specs=(
            P(("rep", "shard"), None),
            P(("rep", "shard"), None),
            P("shard"),
            P("shard"),
            P("shard"),
            P("shard"),
            P("shard", None),
            P("shard"),
            P("shard", None),
            P("shard"),
            P(None, "shard"),
            P("shard"),
            P("shard", None),
            P("shard"),
        ),
        check_vma=False,
    )
```

```python
import functools
import math

import jax
import jax.numpy as jnp
from jax import lax
from jax.experimental import pallas as pl
from jax.experimental.pallas import tpu as pltpu
from jax.sharding import PartitionSpec as P

HD = 64
ROT = 16


epsilon = 1e-05


def norm_rows(values, gain, shift):
    average = jnp.mean(values, axis=-1, keepdims=True)
    centred = values - average
    variance = jnp.mean(centred * centred, axis=-1, keepdims=True)
    return centred * lax.rsqrt(variance + epsilon) * gain + shift


def transposed_right(left, right):
    return lax.dot_general(
        left, right, (((1,), (1,)), ((), ())), preferred_element_type=jnp.float32
    )


def transposed_left(left, right):
    return lax.dot_general(
        left, right, (((0,), (0,)), ((), ())), preferred_element_type=jnp.float32
    )


def exact_gelu(values):
    return jax.nn.gelu(values, approximate=False)


def partner_parts(block, count):
    parts = [block]
    for step in range(1, count):
        pairs = [((index + step) % count, index) for index in range(count)]
        parts.append(lax.ppermute(block, "shard", pairs))
    return parts


def natural(parts, count, mine):
    width = parts[0].shape[1]
    if count == 2:
        return jnp.concatenate(
            [
                jnp.where(mine == 0, parts[0], parts[1]),
                jnp.where(mine == 0, parts[1], parts[0]),
            ],
            axis=1,
        )
    twice = jnp.concatenate(list(parts) + list(parts), axis=1)
    start = lax.rem(count - mine, count) * width
    return lax.dynamic_slice_in_dim(twice, start, count * width, axis=1)


def add_rows(target, target_at, first, first_at, second, rows):
    step = math.gcd(rows, 48)

    def body(turn, carry):
        offset = turn * step
        left = first[pl.ds(pl.multiple_of(first_at + offset, 16), step), :]
        right = second[pl.ds(pl.multiple_of(offset, 16), step), :]
        target[pl.ds(pl.multiple_of(target_at + offset, 16), step), :] = (
            left.astype(jnp.float32) + right.astype(jnp.float32)
        ).astype(target.dtype)
        return carry

    lax.fori_loop(0, rows // step, body, 0)


def sum_kernel(bits, groups, own_ref, other_ref, vec_ref, out_ref, vec_out_ref, *scratch):
    held = scratch[0]
    landing = scratch[1 : 1 + bits]
    vec_held, vec_landing, send_sem, recv_sem, vec_send, vec_recv = scratch[1 + bits :]
    rep = lax.axis_index("rep")
    core = lax.axis_index("shard")
    chunks, rows, _ = out_ref.shape
    sides = [lax.rem(lax.div(rep, 1 << bit), 2) for bit in range(bits)]
    peers = [(rep + (1 << bit) * (1 - 2 * sides[bit]), core) for bit in range(bits)]
    twin = (rep, 1 - core)

    barrier = pltpu.get_barrier_semaphore()
    for device in [twin] + peers:
        pl.semaphore_signal(
            barrier, inc=1, device_id=device, device_id_type=pl.DeviceIdType.MESH
        )
    pl.semaphore_wait(barrier, 1 + bits)

    def order_of(chunk):
        return groups[chunk]

    def region(chunk, depth):
        start = 0
        for place in range(depth):
            start = start + sides[order_of(chunk)[place]] * (rows >> (place + 1))
        return start

    copies = {}

    def launch(chunk, stage, source, target, device):
        copy = pltpu.make_async_remote_copy(
            src_ref=source,
            dst_ref=target,
            send_sem=send_sem.at[chunk, stage],
            recv_sem=recv_sem.at[chunk, stage],
            device_id=device,
            device_id_type=pl.DeviceIdType.MESH,
        )
        copy.start()
        copies[chunk, stage] = copy

    def rows_of(ref, chunk, start, size):
        return ref.at[chunk, pl.ds(pl.multiple_of(start, 16), size), :]

    def advance(chunk, stage):
        if stage == 0:
            launch(chunk, 0, other_ref.at[chunk], held.at[chunk], twin)
            return
        copies[chunk, stage - 1].wait()
        if stage <= bits + 1:
            depth = stage - 1
            size = rows >> depth
            here = region(chunk, depth)
            goal = held if stage <= bits else out_ref
            if depth == 0:
                add_rows(held.at[chunk], 0, held.at[chunk], 0, own_ref.at[chunk], rows)
            else:
                add_rows(
                    goal.at[chunk],
                    here,
                    held.at[chunk],
                    here,
                    landing[depth - 1].at[chunk],
                    size,
                )
        if stage <= bits:
            bit = order_of(chunk)[stage - 1]
            half = rows >> stage
            away = region(chunk, stage - 1) + (1 - sides[bit]) * half
            launch(
                chunk,
                stage,
                rows_of(held, chunk, away, half),
                landing[stage - 1].at[chunk],
                peers[bit],
            )
        elif stage <= 2 * bits:
            depth = 2 * bits + 1 - stage
            bit = order_of(chunk)[depth - 1]
            block = rows_of(out_ref, chunk, region(chunk, depth), rows >> depth)
            launch(chunk, stage, block, block, peers[bit])

    vec_copies = {}

    def advance_vector(stage):
        if stage > 0:
            vec_copies[stage - 1].wait()
            source = vec_ref if stage == 1 else vec_held.at[stage - 2]
            goal = vec_out_ref if stage == bits + 1 else vec_held.at[stage - 1]
            goal[...] = source[...] + vec_landing[stage - 1]
        if stage <= bits:
            copy = pltpu.make_async_remote_copy(
                src_ref=vec_ref if stage == 0 else vec_held.at[stage - 1],
                dst_ref=vec_landing.at[stage],
                send_sem=vec_send.at[stage],
                recv_sem=vec_recv.at[stage],
                device_id=twin if stage == 0 else peers[stage - 1],
                device_id_type=pl.DeviceIdType.MESH,
            )
            copy.start()
            vec_copies[stage] = copy

    turns = []
    for chunk in range(chunks):
        for stage in range(2 * bits + 2):
            turns.append((stage + chunk // 2, chunk, stage))
    for stage in range(bits + 2):
        turns.append((stage, chunks, stage))
    for _, chunk, stage in sorted(turns):
        if chunk == chunks:
            advance_vector(stage)
        else:
            advance(chunk, stage)


def summed(own_rows, other_rows, vector, replicas):
    width = own_rows.shape[1]
    rows = width
    chunks = own_rows.shape[0] // rows
    bits = replicas.bit_length() - 1
    forward = tuple(range(bits))
    swapped = (1, 0) + forward[2:]
    groups = tuple(forward if chunk % 2 == 0 else swapped for chunk in range(chunks))
    stages = 2 * bits + 1
    vmem = pl.BlockSpec(memory_space=pltpu.VMEM)
    landing = [
        pltpu.VMEM((chunks, rows >> (bit + 1), width), jnp.bfloat16) for bit in range(bits)
    ]
    totals, vector_total = pl.pallas_call(
        functools.partial(sum_kernel, bits, groups),
        out_shape=(
            jax.ShapeDtypeStruct((chunks, rows, width), jnp.bfloat16),
            jax.ShapeDtypeStruct(vector.shape, jnp.float32),
        ),
        in_specs=[vmem, pl.BlockSpec(memory_space=pl.ANY), vmem],
        out_specs=(vmem, vmem),
        scratch_shapes=[pltpu.VMEM((chunks, rows, width), jnp.bfloat16)]
        + landing
        + [
            pltpu.VMEM((bits,) + vector.shape, jnp.float32),
            pltpu.VMEM((bits + 1,) + vector.shape, jnp.float32),
            pltpu.SemaphoreType.DMA((chunks, stages)),
            pltpu.SemaphoreType.DMA((chunks, stages)),
            pltpu.SemaphoreType.DMA((bits + 1,)),
            pltpu.SemaphoreType.DMA((bits + 1,)),
        ],
        compiler_params=pltpu.CompilerParams(
            collective_id=0, has_side_effects=True, vmem_limit_bytes=52 * 2**20
        ),
    )(
        own_rows.reshape(chunks, rows, width),
        other_rows.reshape(chunks, rows, width),
        vector,
    )
    return totals.reshape(chunks * rows, width), vector_total


def scattered(gradient, axis):
    owned = lax.psum_scatter(
        gradient.astype(jnp.bfloat16), "shard", scatter_dimension=axis, tiled=True
    )
    return lax.psum(owned, "rep").astype(jnp.float32)


def attention_kernel(
    scale, joined_ref, grad_ref, allowed_ref, tables_ref, mixed_ref, joined_grad_ref
):
    width = mixed_ref.shape[1]
    allowed = allowed_ref[...] > 0.5
    main, rising, falling = tables_ref[0], tables_ref[1], tables_ref[2]
    halfway = ROT // 2
    pair = main.shape[1]

    def turned(block, sign):
        return (
            block * main
            + sign * pltpu.roll(block, halfway, 1) * rising
            + sign * pltpu.roll(block, pair - halfway, 1) * falling
        )

    for begin in range(0, width, pair):
        stop = begin + pair
        queries = turned(joined_ref[:, begin:stop], 1.0).astype(jnp.bfloat16)
        keys = turned(joined_ref[:, width + begin : width + stop], 1.0).astype(jnp.bfloat16)
        rows = joined_ref[:, 2 * width + begin : 2 * width + stop].astype(jnp.bfloat16)
        grads = grad_ref[:, begin:stop]
        mixed, query_grad, key_grad, value_grad = [], [], [], []
        for first in range(0, pair, HD):
            query = queries[:, first : first + HD]
            key = keys[:, first : first + HD]
            value = rows[:, first : first + HD]
            grad = grads[:, first : first + HD]
            scores = jnp.where(allowed, transposed_right(query, key) * scale, -1e30)
            top = jnp.max(scores, axis=-1, keepdims=True)
            exponent = jnp.exp(scores - top)
            probability = exponent / jnp.sum(exponent, axis=-1, keepdims=True)
            low = probability.astype(jnp.bfloat16)
            mixed.append(jnp.dot(low, value, preferred_element_type=jnp.float32))
            prob_grad = transposed_right(grad, value)
            value_grad.append(transposed_left(low, grad))
            inner = jnp.sum(prob_grad * probability, axis=-1, keepdims=True)
            score_grad = (probability * (prob_grad - inner)).astype(jnp.bfloat16)
            query_grad.append(jnp.dot(score_grad, key, preferred_element_type=jnp.float32))
            key_grad.append(transposed_left(score_grad, query))
        mixed_ref[:, begin:stop] = jnp.concatenate(mixed, axis=1).astype(jnp.bfloat16)
        query_block = turned(jnp.concatenate(query_grad, axis=1) * scale, -1.0)
        key_block = turned(jnp.concatenate(key_grad, axis=1) * scale, -1.0)
        value_block = jnp.concatenate(value_grad, axis=1)
        joined_grad_ref[:, begin:stop] = query_block.astype(jnp.bfloat16)
        joined_grad_ref[:, width + begin : width + stop] = key_block.astype(jnp.bfloat16)
        joined_grad_ref[:, 2 * width + begin : 2 * width + stop] = value_block.astype(
            jnp.bfloat16
        )


def attended(joined, mixed_grad, allowed, cosine, sine):
    rows, width = mixed_grad.shape
    plain = jnp.ones((rows, HD - ROT), jnp.float32)
    none = jnp.zeros((rows, HD - ROT), jnp.float32)
    blank = jnp.zeros_like(sine)
    tables = jnp.stack(
        [
            jnp.concatenate([cosine, cosine, plain] * 2, axis=1),
            jnp.concatenate([blank, sine, none] * 2, axis=1),
            jnp.concatenate([-sine, blank, none] * 2, axis=1),
        ]
    )
    vmem = pl.BlockSpec(memory_space=pltpu.VMEM)
    return pl.pallas_call(
        functools.partial(attention_kernel, 1.0 / math.sqrt(HD)),
        out_shape=(
            jax.ShapeDtypeStruct((rows, width), jnp.bfloat16),
            jax.ShapeDtypeStruct((rows, 3 * width), jnp.bfloat16),
        ),
        in_specs=[vmem] * 4,
        out_specs=(vmem, vmem),
        compiler_params=pltpu.CompilerParams(vmem_limit_bytes=40 * 2**20),
        cost_estimate=pl.CostEstimate(
            flops=14 * rows * rows * width,
            bytes_accessed=10 * 2**20,
            transcendentals=rows * rows * width // HD,
        ),
    )(joined, mixed_grad, allowed.astype(jnp.float32), tables)


def make_shards(replicas, count):
    def shards(
        hidden_in,
        cotangent,
        token_count,
        segment_ids,
        positions,
        first_gain,
        first_shift,
        second_gain,
        second_shift,
        input_weight,
        input_bias,
        output_weight,
        output_bias,
        expand_weight,
        expand_bias,
        reduce_weight,
        reduce_bias,
    ):
        row_count = hidden_in.shape[0]
        mine = lax.axis_index("shard")
        replica = lax.axis_index("rep")
        own = hidden_in.shape[1] // count
        owned_vectors = [
            first_gain,
            first_shift,
            second_gain,
            second_shift,
            input_bias,
            output_bias,
            reduce_bias,
            expand_bias,
        ]
        vector_sizes = [vector.shape[0] for vector in owned_vectors]
        vector_parts = partner_parts(jnp.concatenate(owned_vectors)[None, :], count)
        wide_parts = partner_parts(expand_weight, count)
        narrow_parts = partner_parts(reduce_weight, count)
        joint_parts = partner_parts(input_weight, count)
        proj_parts = partner_parts(output_weight, count)

        def vector_of(place):
            begin = sum(vector_sizes[:place])
            pieces = [part[:, begin : begin + vector_sizes[place]] for part in vector_parts]
            return pieces

        whole_vectors = [natural(vector_of(place), count, mine)[0] for place in range(7)]
        (
            gain_one,
            shift_one,
            gain_two,
            shift_two,
            joint_bias,
            proj_bias,
            narrow_bias,
        ) = [vector.astype(jnp.float32) for vector in whole_vectors]
        wide_bias_parts = [piece.astype(jnp.float32) for piece in vector_of(7)]

        values = hidden_in.astype(jnp.float32)
        slot_index = jnp.arange(row_count)
        live_rows = slot_index < token_count[0]
        live_mask = live_rows.astype(jnp.float32)[:, None]
        normed_one, first_pull = jax.vjp(norm_rows, values, gain_one, shift_one)
        normed_two, second_pull = jax.vjp(norm_rows, values, gain_two, shift_two)
        first_low = normed_one.astype(jnp.bfloat16)
        second_low = normed_two.astype(jnp.bfloat16)
        grad_rows = cotangent.astype(jnp.float32) * live_mask
        grad_low = grad_rows.astype(jnp.bfloat16)
        bias_sum = jnp.sum(grad_rows, axis=0)

        width = hidden_in.shape[1]
        paired = count == 2 and replicas >= 4 and width % (16 * replicas) == 0
        paired = paired and replicas & (replicas - 1) == 0

        def stacked(left, right):
            return [
                transposed_left(left, right[:, begin : begin + width]).astype(jnp.bfloat16)
                for begin in range(0, right.shape[1], width)
            ]

        forward_feed = narrow_bias[None, :]
        activated_parts = []
        expanded_grad_parts = []
        second_grad = None
        for wide, narrow, bias in zip(wide_parts, narrow_parts, wide_bias_parts):
            expanded = jnp.dot(second_low, wide, preferred_element_type=jnp.float32) + bias
            activated_full, expand_pull = jax.vjp(exact_gelu, expanded)
            activated = activated_full.astype(jnp.bfloat16)
            forward_feed = forward_feed + jnp.dot(
                activated, narrow, preferred_element_type=jnp.float32
            )
            hidden_grad = transposed_right(grad_low, narrow)
            expanded_grad = expand_pull(hidden_grad)[0].astype(jnp.bfloat16)
            part_grad = transposed_right(expanded_grad, wide)
            second_grad = part_grad if second_grad is None else second_grad + part_grad
            activated_parts.append(activated)
            expanded_grad_parts.append(expanded_grad)
        wide_bias_grad = natural(
            [
                jnp.sum(part, axis=0, dtype=jnp.float32)[None, :]
                for part in expanded_grad_parts
            ],
            count,
            mine,
        )[0]

        def feature_parts(block):
            if count == 2:
                lower, upper = block[:, :own], block[:, own:]
                return [
                    jnp.where(mine == 0, lower, upper),
                    jnp.where(mine == 0, upper, lower),
                ]
            return [
                lax.dynamic_slice_in_dim(
                    block, lax.rem(mine + step, count) * own, own, axis=1
                )
                for step in range(count)
            ]

        first_parts = feature_parts(first_low)
        joined = joint_bias[None, :]
        for part, weight in zip(first_parts, joint_parts):
            joined = joined + jnp.dot(part, weight, preferred_element_type=jnp.float32)
        halfway = ROT // 2
        frequency = 10000.0 ** (-jnp.arange(halfway, dtype=jnp.float32) * 2.0 / ROT)
        angles = positions.astype(jnp.float32)[:, None] * frequency[None, :]
        cosine_table = jnp.cos(angles)
        sine_table = jnp.sin(angles)
        allowed = (
            (segment_ids[:, None] == segment_ids[None, :])
            & (slot_index[None, :] <= slot_index[:, None])
            & live_rows[None, :]
        )
        allowed = allowed | (slot_index[:, None] == slot_index[None, :])
        mixed_grad = natural(
            [transposed_right(grad_low, weight).astype(jnp.bfloat16) for weight in proj_parts],
            count,
            mine,
        )
        mixed_low, joined_grad = attended(joined, mixed_grad, allowed, cosine_table, sine_table)
        mixed_parts = feature_parts(mixed_low)
        attention = proj_bias[None, :]
        for part, weight in zip(mixed_parts, proj_parts):
            attention = attention + jnp.dot(part, weight, preferred_element_type=jnp.float32)
        block_output = (live_mask * (values + attention + forward_feed)).astype(jnp.bfloat16)
        joint_bias_grad = jnp.sum(joined_grad, axis=0, dtype=jnp.float32)
        first_grad = natural(
            [transposed_right(joined_grad, weight) for weight in joint_parts], count, mine
        )
        first_input, gain_one_grad, shift_one_grad = first_pull(first_grad)
        second_input, gain_two_grad, shift_two_grad = second_pull(second_grad)
        input_gradient = grad_rows + first_input + second_input
        sums = [
            gain_one_grad,
            shift_one_grad,
            gain_two_grad,
            shift_two_grad,
            joint_bias_grad,
            bias_sum,
            wide_bias_grad,
        ]
        sum_sizes = [item.shape[0] for item in sums]
        joined_sums = jnp.concatenate(sums).reshape(-1, 128)
        if paired:
            sent = [
                jnp.concatenate(
                    stacked(activated_parts[part], grad_low)
                    + stacked(second_low, expanded_grad_parts[part])
                    + stacked(first_parts[part], joined_grad)
                    + stacked(mixed_parts[part], grad_low),
                    axis=0,
                )
                for part in range(count)
            ]
            totals, joined_sums = summed(sent[0], sent[1], joined_sums, replicas)
            place = 0

            def taken(tall, broad):
                nonlocal place
                pieces = []
                for _ in range(broad // width):
                    pieces.append(totals[place : place + tall])
                    place += tall
                pieces = [piece.astype(jnp.float32) for piece in pieces]
                return pieces[0] if len(pieces) == 1 else jnp.concatenate(pieces, axis=1)

            total_narrow = taken(*reduce_weight.shape)
            total_wide = taken(*expand_weight.shape)
            total_joint = taken(*input_weight.shape)
            total_proj = taken(*output_weight.shape)
        else:
            activated = natural(activated_parts, count, mine)
            expanded_grad = natural(expanded_grad_parts, count, mine)
            total_narrow = scattered(transposed_left(activated, grad_low), 0)
            total_wide = scattered(transposed_left(second_low, expanded_grad), 1)
            total_joint = scattered(transposed_left(first_low, joined_grad), 0)
            total_proj = scattered(transposed_left(mixed_low, grad_low), 0)
            joined_sums = lax.psum(joined_sums, ("rep", "shard"))
        joined_sums = joined_sums.reshape(-1)
        owned = []
        begin = 0
        for size in sum_sizes:
            share = size // count
            owned.append(
                lax.dynamic_slice_in_dim(joined_sums, begin + mine * share, share, axis=0)
            )
            begin += size
        return (
            block_output,
            input_gradient,
            owned[0],
            owned[1],
            owned[2],
            owned[3],
            total_joint,
            owned[4],
            total_proj,
            owned[5],
            total_wide,
            owned[6],
            total_narrow,
            owned[5],
        )

    return shards


def solution(mesh):
    return jax.shard_map(
        make_shards(mesh.shape["rep"], mesh.shape["shard"]),
        mesh=mesh,
        in_specs=(
            P(("rep", "shard"), None),
            P(("rep", "shard"), None),
            P(("rep", "shard")),
            P(("rep", "shard")),
            P(("rep", "shard")),
            P("shard"),
            P("shard"),
            P("shard"),
            P("shard"),
            P("shard", None),
            P("shard"),
            P("shard", None),
            P("shard"),
            P(None, "shard"),
            P("shard"),
            P("shard", None),
            P("shard"),
        ),
        out_specs=(
            P(("rep", "shard"), None),
            P(("rep", "shard"), None),
            P("shard"),
            P("shard"),
            P("shard"),
            P("shard"),
            P("shard", None),
            P("shard"),
            P("shard", None),
            P("shard"),
            P(None, "shard"),
            P("shard"),
            P("shard", None),
            P("shard"),
        ),
        check_vma=False,
    )
```

```python
import functools
import math

import jax
import jax.numpy as jnp
from jax import lax
from jax.experimental import pallas as pl
from jax.experimental.pallas import tpu as pltpu
from jax.sharding import PartitionSpec as P

HD = 64
ROT = 16


epsilon = 1e-05


def norm_rows(values, gain, shift):
    average = jnp.mean(values, axis=-1, keepdims=True)
    centred = values - average
    variance = jnp.mean(centred * centred, axis=-1, keepdims=True)
    return centred * lax.rsqrt(variance + epsilon) * gain + shift


def transposed_right(left, right):
    return lax.dot_general(
        left, right, (((1,), (1,)), ((), ())), preferred_element_type=jnp.float32
    )


def transposed_left(left, right):
    return lax.dot_general(
        left, right, (((0,), (0,)), ((), ())), preferred_element_type=jnp.float32
    )


def exact_gelu(values):
    return jax.nn.gelu(values, approximate=False)


def partner_parts(block, count):
    parts = [block]
    for step in range(1, count):
        pairs = [((index + step) % count, index) for index in range(count)]
        parts.append(lax.ppermute(block, "shard", pairs))
    return parts


def natural(parts, count, mine):
    width = parts[0].shape[1]
    if count == 2:
        return jnp.concatenate(
            [
                jnp.where(mine == 0, parts[0], parts[1]),
                jnp.where(mine == 0, parts[1], parts[0]),
            ],
            axis=1,
        )
    twice = jnp.concatenate(list(parts) + list(parts), axis=1)
    start = lax.rem(count - mine, count) * width
    return lax.dynamic_slice_in_dim(twice, start, count * width, axis=1)


def add_rows(target, target_at, first, first_at, second, rows):
    step = math.gcd(rows, 48)

    def body(turn, carry):
        offset = turn * step
        left = first[pl.ds(pl.multiple_of(first_at + offset, 16), step), :]
        right = second[pl.ds(pl.multiple_of(offset, 16), step), :]
        target[pl.ds(pl.multiple_of(target_at + offset, 16), step), :] = (
            left.astype(jnp.float32) + right.astype(jnp.float32)
        ).astype(target.dtype)
        return carry

    lax.fori_loop(0, rows // step, body, 0)


def sum_kernel(bits, groups, own_ref, other_ref, vec_ref, out_ref, vec_out_ref, *scratch):
    held = scratch[0]
    landing = scratch[1 : 1 + bits]
    vec_held, vec_landing, send_sem, recv_sem, vec_send, vec_recv = scratch[1 + bits :]
    rep = lax.axis_index("rep")
    core = lax.axis_index("shard")
    chunks, rows, _ = out_ref.shape
    sides = [lax.rem(lax.div(rep, 1 << bit), 2) for bit in range(bits)]
    peers = [(rep + (1 << bit) * (1 - 2 * sides[bit]), core) for bit in range(bits)]
    twin = (rep, 1 - core)

    barrier = pltpu.get_barrier_semaphore()
    for device in [twin] + peers:
        pl.semaphore_signal(
            barrier, inc=1, device_id=device, device_id_type=pl.DeviceIdType.MESH
        )
    pl.semaphore_wait(barrier, 1 + bits)

    def order_of(chunk):
        return groups[chunk]

    def region(chunk, depth):
        start = 0
        for place in range(depth):
            start = start + sides[order_of(chunk)[place]] * (rows >> (place + 1))
        return start

    copies = {}

    def launch(chunk, stage, source, target, device):
        copy = pltpu.make_async_remote_copy(
            src_ref=source,
            dst_ref=target,
            send_sem=send_sem.at[chunk, stage],
            recv_sem=recv_sem.at[chunk, stage],
            device_id=device,
            device_id_type=pl.DeviceIdType.MESH,
        )
        copy.start()
        copies[chunk, stage] = copy

    def rows_of(ref, chunk, start, size):
        return ref.at[chunk, pl.ds(pl.multiple_of(start, 16), size), :]

    def advance(chunk, stage):
        if stage == 0:
            launch(chunk, 0, other_ref.at[chunk], held.at[chunk], twin)
            return
        copies[chunk, stage - 1].wait()
        if stage <= bits + 1:
            depth = stage - 1
            size = rows >> depth
            here = region(chunk, depth)
            goal = held if stage <= bits else out_ref
            if depth == 0:
                add_rows(held.at[chunk], 0, held.at[chunk], 0, own_ref.at[chunk], rows)
            else:
                add_rows(
                    goal.at[chunk],
                    here,
                    held.at[chunk],
                    here,
                    landing[depth - 1].at[chunk],
                    size,
                )
        if stage <= bits:
            bit = order_of(chunk)[stage - 1]
            half = rows >> stage
            away = region(chunk, stage - 1) + (1 - sides[bit]) * half
            launch(
                chunk,
                stage,
                rows_of(held, chunk, away, half),
                landing[stage - 1].at[chunk],
                peers[bit],
            )
        elif stage <= 2 * bits:
            depth = 2 * bits + 1 - stage
            bit = order_of(chunk)[depth - 1]
            block = rows_of(out_ref, chunk, region(chunk, depth), rows >> depth)
            launch(chunk, stage, block, block, peers[bit])

    vec_copies = {}

    def advance_vector(stage):
        if stage > 0:
            vec_copies[stage - 1].wait()
            source = vec_ref if stage == 1 else vec_held.at[stage - 2]
            goal = vec_out_ref if stage == bits + 1 else vec_held.at[stage - 1]
            goal[...] = source[...] + vec_landing[stage - 1]
        if stage <= bits:
            copy = pltpu.make_async_remote_copy(
                src_ref=vec_ref if stage == 0 else vec_held.at[stage - 1],
                dst_ref=vec_landing.at[stage],
                send_sem=vec_send.at[stage],
                recv_sem=vec_recv.at[stage],
                device_id=twin if stage == 0 else peers[stage - 1],
                device_id_type=pl.DeviceIdType.MESH,
            )
            copy.start()
            vec_copies[stage] = copy

    turns = []
    for chunk in range(chunks):
        for stage in range(2 * bits + 2):
            turns.append((stage, chunk, stage))
    for stage in range(bits + 2):
        turns.append((stage, chunks, stage))
    for _, chunk, stage in sorted(turns):
        if chunk == chunks:
            advance_vector(stage)
        else:
            advance(chunk, stage)


def summed(own_rows, other_rows, vector, replicas):
    width = own_rows.shape[1]
    rows = width
    chunks = own_rows.shape[0] // rows
    bits = replicas.bit_length() - 1
    forward = tuple(range(bits))
    swapped = (1, 0) + forward[2:]
    groups = tuple(forward if chunk % 2 == 0 else swapped for chunk in range(chunks))
    stages = 2 * bits + 1
    vmem = pl.BlockSpec(memory_space=pltpu.VMEM)
    landing = [
        pltpu.VMEM((chunks, rows >> (bit + 1), width), jnp.bfloat16) for bit in range(bits)
    ]
    totals, vector_total = pl.pallas_call(
        functools.partial(sum_kernel, bits, groups),
        out_shape=(
            jax.ShapeDtypeStruct((chunks, rows, width), jnp.bfloat16),
            jax.ShapeDtypeStruct(vector.shape, jnp.float32),
        ),
        in_specs=[vmem, pl.BlockSpec(memory_space=pl.ANY), vmem],
        out_specs=(vmem, vmem),
        scratch_shapes=[pltpu.VMEM((chunks, rows, width), jnp.bfloat16)]
        + landing
        + [
            pltpu.VMEM((bits,) + vector.shape, jnp.float32),
            pltpu.VMEM((bits + 1,) + vector.shape, jnp.float32),
            pltpu.SemaphoreType.DMA((chunks, stages)),
            pltpu.SemaphoreType.DMA((chunks, stages)),
            pltpu.SemaphoreType.DMA((bits + 1,)),
            pltpu.SemaphoreType.DMA((bits + 1,)),
        ],
        compiler_params=pltpu.CompilerParams(
            collective_id=0, has_side_effects=True, vmem_limit_bytes=52 * 2**20
        ),
    )(
        own_rows.reshape(chunks, rows, width),
        other_rows.reshape(chunks, rows, width),
        vector,
    )
    return totals.reshape(chunks * rows, width), vector_total


def scattered(gradient, axis):
    owned = lax.psum_scatter(
        gradient.astype(jnp.bfloat16), "shard", scatter_dimension=axis, tiled=True
    )
    return lax.psum(owned, "rep").astype(jnp.float32)


def attention_kernel(
    scale, joined_ref, grad_ref, allowed_ref, tables_ref, mixed_ref, joined_grad_ref
):
    width = mixed_ref.shape[1]
    allowed = allowed_ref[...] > 0.5
    main, rising, falling = tables_ref[0], tables_ref[1], tables_ref[2]
    halfway = ROT // 2
    pair = main.shape[1]

    def turned(block, sign):
        return (
            block * main
            + sign * pltpu.roll(block, halfway, 1) * rising
            + sign * pltpu.roll(block, pair - halfway, 1) * falling
        )

    for begin in range(0, width, pair):
        stop = begin + pair
        queries = turned(joined_ref[:, begin:stop], 1.0).astype(jnp.bfloat16)
        keys = turned(joined_ref[:, width + begin : width + stop], 1.0).astype(jnp.bfloat16)
        rows = joined_ref[:, 2 * width + begin : 2 * width + stop].astype(jnp.bfloat16)
        grads = grad_ref[:, begin:stop]
        mixed, query_grad, key_grad, value_grad = [], [], [], []
        for first in range(0, pair, HD):
            query = queries[:, first : first + HD]
            key = keys[:, first : first + HD]
            value = rows[:, first : first + HD]
            grad = grads[:, first : first + HD]
            scores = jnp.where(allowed, transposed_right(query, key) * scale, -1e30)
            top = jnp.max(scores, axis=-1, keepdims=True)
            exponent = jnp.exp(scores - top)
            probability = exponent / jnp.sum(exponent, axis=-1, keepdims=True)
            low = probability.astype(jnp.bfloat16)
            mixed.append(jnp.dot(low, value, preferred_element_type=jnp.float32))
            prob_grad = transposed_right(grad, value)
            value_grad.append(transposed_left(low, grad))
            inner = jnp.sum(prob_grad * probability, axis=-1, keepdims=True)
            score_grad = (probability * (prob_grad - inner)).astype(jnp.bfloat16)
            query_grad.append(jnp.dot(score_grad, key, preferred_element_type=jnp.float32))
            key_grad.append(transposed_left(score_grad, query))
        mixed_ref[:, begin:stop] = jnp.concatenate(mixed, axis=1).astype(jnp.bfloat16)
        query_block = turned(jnp.concatenate(query_grad, axis=1) * scale, -1.0)
        key_block = turned(jnp.concatenate(key_grad, axis=1) * scale, -1.0)
        value_block = jnp.concatenate(value_grad, axis=1)
        joined_grad_ref[:, begin:stop] = query_block.astype(jnp.bfloat16)
        joined_grad_ref[:, width + begin : width + stop] = key_block.astype(jnp.bfloat16)
        joined_grad_ref[:, 2 * width + begin : 2 * width + stop] = value_block.astype(
            jnp.bfloat16
        )


def attended(joined, mixed_grad, allowed, cosine, sine):
    rows, width = mixed_grad.shape
    plain = jnp.ones((rows, HD - ROT), jnp.float32)
    none = jnp.zeros((rows, HD - ROT), jnp.float32)
    blank = jnp.zeros_like(sine)
    tables = jnp.stack(
        [
            jnp.concatenate([cosine, cosine, plain] * 2, axis=1),
            jnp.concatenate([blank, sine, none] * 2, axis=1),
            jnp.concatenate([-sine, blank, none] * 2, axis=1),
        ]
    )
    vmem = pl.BlockSpec(memory_space=pltpu.VMEM)
    return pl.pallas_call(
        functools.partial(attention_kernel, 1.0 / math.sqrt(HD)),
        out_shape=(
            jax.ShapeDtypeStruct((rows, width), jnp.bfloat16),
            jax.ShapeDtypeStruct((rows, 3 * width), jnp.bfloat16),
        ),
        in_specs=[vmem] * 4,
        out_specs=(vmem, vmem),
        compiler_params=pltpu.CompilerParams(vmem_limit_bytes=40 * 2**20),
        cost_estimate=pl.CostEstimate(
            flops=14 * rows * rows * width,
            bytes_accessed=10 * 2**20,
            transcendentals=rows * rows * width // HD,
        ),
    )(joined, mixed_grad, allowed.astype(jnp.float32), tables)


def make_shards(replicas, count):
    def shards(
        hidden_in,
        cotangent,
        token_count,
        segment_ids,
        positions,
        first_gain,
        first_shift,
        second_gain,
        second_shift,
        input_weight,
        input_bias,
        output_weight,
        output_bias,
        expand_weight,
        expand_bias,
        reduce_weight,
        reduce_bias,
    ):
        row_count = hidden_in.shape[0]
        mine = lax.axis_index("shard")
        replica = lax.axis_index("rep")
        own = hidden_in.shape[1] // count
        owned_vectors = [
            first_gain,
            first_shift,
            second_gain,
            second_shift,
            input_bias,
            output_bias,
            reduce_bias,
            expand_bias,
        ]
        vector_sizes = [vector.shape[0] for vector in owned_vectors]
        vector_parts = partner_parts(jnp.concatenate(owned_vectors)[None, :], count)
        wide_parts = partner_parts(expand_weight, count)
        narrow_parts = partner_parts(reduce_weight, count)
        joint_parts = partner_parts(input_weight, count)
        proj_parts = partner_parts(output_weight, count)

        def vector_of(place):
            begin = sum(vector_sizes[:place])
            pieces = [part[:, begin : begin + vector_sizes[place]] for part in vector_parts]
            return pieces

        whole_vectors = [natural(vector_of(place), count, mine)[0] for place in range(7)]
        (
            gain_one,
            shift_one,
            gain_two,
            shift_two,
            joint_bias,
            proj_bias,
            narrow_bias,
        ) = [vector.astype(jnp.float32) for vector in whole_vectors]
        wide_bias_parts = [piece.astype(jnp.float32) for piece in vector_of(7)]

        values = hidden_in.astype(jnp.float32)
        slot_index = jnp.arange(row_count)
        live_rows = slot_index < token_count[0]
        live_mask = live_rows.astype(jnp.float32)[:, None]
        normed_one, first_pull = jax.vjp(norm_rows, values, gain_one, shift_one)
        normed_two, second_pull = jax.vjp(norm_rows, values, gain_two, shift_two)
        first_low = normed_one.astype(jnp.bfloat16)
        second_low = normed_two.astype(jnp.bfloat16)
        grad_rows = cotangent.astype(jnp.float32) * live_mask
        grad_low = grad_rows.astype(jnp.bfloat16)
        bias_sum = jnp.sum(grad_rows, axis=0)

        width = hidden_in.shape[1]
        paired = count == 2 and replicas >= 4 and width % (16 * replicas) == 0
        paired = paired and replicas & (replicas - 1) == 0

        def stacked(left, right):
            return [
                transposed_left(left, right[:, begin : begin + width]).astype(jnp.bfloat16)
                for begin in range(0, right.shape[1], width)
            ]

        forward_feed = narrow_bias[None, :]
        activated_parts = []
        expanded_grad_parts = []
        second_grad = None
        for wide, narrow, bias in zip(wide_parts, narrow_parts, wide_bias_parts):
            expanded = jnp.dot(second_low, wide, preferred_element_type=jnp.float32) + bias
            activated_full, expand_pull = jax.vjp(exact_gelu, expanded)
            activated = activated_full.astype(jnp.bfloat16)
            forward_feed = forward_feed + jnp.dot(
                activated, narrow, preferred_element_type=jnp.float32
            )
            hidden_grad = transposed_right(grad_low, narrow)
            expanded_grad = expand_pull(hidden_grad)[0].astype(jnp.bfloat16)
            part_grad = transposed_right(expanded_grad, wide)
            second_grad = part_grad if second_grad is None else second_grad + part_grad
            activated_parts.append(activated)
            expanded_grad_parts.append(expanded_grad)
        wide_bias_grad = natural(
            [
                jnp.sum(part, axis=0, dtype=jnp.float32)[None, :]
                for part in expanded_grad_parts
            ],
            count,
            mine,
        )[0]

        def feature_parts(block):
            if count == 2:
                lower, upper = block[:, :own], block[:, own:]
                return [
                    jnp.where(mine == 0, lower, upper),
                    jnp.where(mine == 0, upper, lower),
                ]
            return [
                lax.dynamic_slice_in_dim(
                    block, lax.rem(mine + step, count) * own, own, axis=1
                )
                for step in range(count)
            ]

        first_parts = feature_parts(first_low)
        joined = joint_bias[None, :]
        for part, weight in zip(first_parts, joint_parts):
            joined = joined + jnp.dot(part, weight, preferred_element_type=jnp.float32)
        halfway = ROT // 2
        frequency = 10000.0 ** (-jnp.arange(halfway, dtype=jnp.float32) * 2.0 / ROT)
        angles = positions.astype(jnp.float32)[:, None] * frequency[None, :]
        cosine_table = jnp.cos(angles)
        sine_table = jnp.sin(angles)
        allowed = (
            (segment_ids[:, None] == segment_ids[None, :])
            & (slot_index[None, :] <= slot_index[:, None])
            & live_rows[None, :]
        )
        allowed = allowed | (slot_index[:, None] == slot_index[None, :])
        mixed_grad = natural(
            [transposed_right(grad_low, weight).astype(jnp.bfloat16) for weight in proj_parts],
            count,
            mine,
        )
        mixed_low, joined_grad = attended(joined, mixed_grad, allowed, cosine_table, sine_table)
        mixed_parts = feature_parts(mixed_low)
        attention = proj_bias[None, :]
        for part, weight in zip(mixed_parts, proj_parts):
            attention = attention + jnp.dot(part, weight, preferred_element_type=jnp.float32)
        block_output = (live_mask * (values + attention + forward_feed)).astype(jnp.bfloat16)
        joint_bias_grad = jnp.sum(joined_grad, axis=0, dtype=jnp.float32)
        first_grad = natural(
            [transposed_right(joined_grad, weight) for weight in joint_parts], count, mine
        )
        first_input, gain_one_grad, shift_one_grad = first_pull(first_grad)
        second_input, gain_two_grad, shift_two_grad = second_pull(second_grad)
        input_gradient = grad_rows + first_input + second_input
        sums = [
            gain_one_grad,
            shift_one_grad,
            gain_two_grad,
            shift_two_grad,
            joint_bias_grad,
            bias_sum,
            wide_bias_grad,
        ]
        sum_sizes = [item.shape[0] for item in sums]
        joined_sums = jnp.concatenate(sums).reshape(-1, 128)
        if paired:
            sent = [
                jnp.concatenate(
                    stacked(activated_parts[part], grad_low)
                    + stacked(second_low, expanded_grad_parts[part])
                    + stacked(first_parts[part], joined_grad)
                    + stacked(mixed_parts[part], grad_low),
                    axis=0,
                )
                for part in range(count)
            ]
            totals, joined_sums = summed(sent[0], sent[1], joined_sums, replicas)
            place = 0

            def taken(tall, broad):
                nonlocal place
                pieces = []
                for _ in range(broad // width):
                    pieces.append(totals[place : place + tall])
                    place += tall
                pieces = [piece.astype(jnp.float32) for piece in pieces]
                return pieces[0] if len(pieces) == 1 else jnp.concatenate(pieces, axis=1)

            total_narrow = taken(*reduce_weight.shape)
            total_wide = taken(*expand_weight.shape)
            total_joint = taken(*input_weight.shape)
            total_proj = taken(*output_weight.shape)
        else:
            activated = natural(activated_parts, count, mine)
            expanded_grad = natural(expanded_grad_parts, count, mine)
            total_narrow = scattered(transposed_left(activated, grad_low), 0)
            total_wide = scattered(transposed_left(second_low, expanded_grad), 1)
            total_joint = scattered(transposed_left(first_low, joined_grad), 0)
            total_proj = scattered(transposed_left(mixed_low, grad_low), 0)
            joined_sums = lax.psum(joined_sums, ("rep", "shard"))
        joined_sums = joined_sums.reshape(-1)
        owned = []
        begin = 0
        for size in sum_sizes:
            share = size // count
            owned.append(
                lax.dynamic_slice_in_dim(joined_sums, begin + mine * share, share, axis=0)
            )
            begin += size
        return (
            block_output,
            input_gradient,
            owned[0],
            owned[1],
            owned[2],
            owned[3],
            total_joint,
            owned[4],
            total_proj,
            owned[5],
            total_wide,
            owned[6],
            total_narrow,
            owned[5],
        )

    return shards


def solution(mesh):
    return jax.shard_map(
        make_shards(mesh.shape["rep"], mesh.shape["shard"]),
        mesh=mesh,
        in_specs=(
            P(("rep", "shard"), None),
            P(("rep", "shard"), None),
            P(("rep", "shard")),
            P(("rep", "shard")),
            P(("rep", "shard")),
            P("shard"),
            P("shard"),
            P("shard"),
            P("shard"),
            P("shard", None),
            P("shard"),
            P("shard", None),
            P("shard"),
            P(None, "shard"),
            P("shard"),
            P("shard", None),
            P("shard"),
        ),
        out_specs=(
            P(("rep", "shard"), None),
            P(("rep", "shard"), None),
            P("shard"),
            P("shard"),
            P("shard"),
            P("shard"),
            P("shard", None),
            P("shard"),
            P("shard", None),
            P("shard"),
            P(None, "shard"),
            P("shard"),
            P("shard", None),
            P("shard"),
        ),
        check_vma=False,
    )
```
